256 devices in a mesh: row: 32 (over y, z_hi, x), col: 8 (over z_lo, core).
Axes of the slice: x: 4, y: 4, z: 8 (z_hi: 2, z_lo: 4; z = z_hi * 4 + z_lo), core: 2. Of those that a mesh axis runs over, the one named last changes fastest.
Arguments:
- pair: bfloat16 [512, 512, 128], P('row', 'col'), may hold values from -6 to 6
- token_mask: int32 [512], replicated, may hold values 0 or 1
- ln_in_gain: float32 [128], replicated, may hold values from 0.25 to 1.75
- ln_in_bias: float32 [128], replicated, may hold values from -3 to 3
- w_left: bfloat16 [128, 128], replicated, may hold values from -0.5 to 0.5
- w_left_gate: bfloat16 [128, 128], replicated, may hold values from -0.5 to 0.5
- w_right: bfloat16 [128, 128], replicated, may hold values from -0.5 to 0.5
- w_right_gate: bfloat16 [128, 128], replicated, may hold values from -0.5 to 0.5
- w_gate: bfloat16 [128, 128], replicated, may hold values from -0.5 to 0.5
- ln_out_gain: float32 [128], replicated, may hold values from 0.25 to 1.75
- ln_out_bias: float32 [128], replicated, may hold values from -3 to 3
- w_out: bfloat16 [128, 128], replicated, may hold values from -0.5 to 0.5
Outputs:
- update: bfloat16 [512, 512, 128], P('row', 'col')
The draws below stay inside these ranges and needn't reach their ends.
All inputs are finite; a program needn't handle non-finite values.
Results may differ from the reference program's by a relative error of at most 0.0054.
Values may be sent and summed in bfloat16 or wider, within the bound.
No kernel may reach another device: no remote copies, remote signals or barrier semaphores. Data moves between devices by JAX's collectives and lax.ppermute only.
A program may use at most 64 MiB of HBM per device.

```python
import math
import jax
import jax.numpy as jnp
from jax import lax

C = 128
HID = 128
TOKENS = 512


def signed_table(key):
    perm_key, sign_key, jitter_key = jax.random.split(key, 3)
    row_order = jax.random.permutation(perm_key, C).astype(jnp.int32)
    column_ids = jnp.arange(HID, dtype=jnp.int32)
    common_bits = row_order[:, None] & column_ids[None, :]
    parity_sum = jnp.zeros((C, HID), jnp.int32)
    for bit_place in range(16):
        parity_sum = parity_sum + (common_bits >> bit_place & 1)
    sign_table = 1 - 2 * (parity_sum % 2)
    column_signs = 2 * jax.random.randint(sign_key, (HID,), 0, 2) - 1
    signed_base = (sign_table * column_signs[None, :]).astype(jnp.float32) / math.sqrt(C)
    jitter = jnp.clip(jax.random.normal(jitter_key, (C, HID), jnp.float32), -3.0, 3.0) * (0.1 / math.sqrt(C))
    return (signed_base + jitter).astype(jnp.bfloat16)


def draw_w_left(key, part):
    key = jax.random.fold_in(key, 21)
    return signed_table(key)


def draw_w_left_gate(key, part):
    key = jax.random.fold_in(key, 22)
    return signed_table(key)


def draw_w_right(key, part):
    key = jax.random.fold_in(key, 23)
    return signed_table(key)


def draw_w_right_gate(key, part):
    key = jax.random.fold_in(key, 24)
    return signed_table(key)


def draw_pair(key, part):
    key = jax.random.fold_in(key, 11)
    drawn = jnp.clip(jax.random.normal(key, (TOKENS, TOKENS, C), jnp.float32), -6.0, 6.0)
    return drawn.astype(jnp.bfloat16)


def touch_ends(result, key, smallest, top_value):
    extent = result.shape
    index_at = [jax.random.randint(jax.random.fold_in(key, axis), (), 0, extent[axis]) for axis in range(len(extent))]
    result = result.at[tuple(index_at)].set(smallest)
    longest = extent.index(max(extent))
    index_at[longest] = (index_at[longest] + 1) % extent[longest]
    return result.at[tuple(index_at)].set(top_value)


def noise(own_key, dims, spread, most, kind=jnp.bfloat16):
    values = jax.random.normal(own_key, dims, jnp.float32) * spread
    return jnp.minimum(jnp.maximum(values, -most), most).astype(kind)


def setup_inputs(seed: int = 0) -> dict:
    arg_keys = jax.random.split(jax.random.key(seed), 13)
    return {
        "pair": draw_pair(jax.random.fold_in(arg_keys[12], 71), 0),
        "token_mask": touch_ends((jax.random.randint(arg_keys[1], (TOKENS,), 0, 8) < 7).astype(jnp.int32), jax.random.fold_in(arg_keys[1], 1), 0, 1),
        "ln_in_gain": jnp.clip(1.0 + 0.15 * jax.random.normal(arg_keys[2], (C,), jnp.float32), 0.25, 1.75),
        "ln_in_bias": noise(arg_keys[3], (C,), 0.5, 3.0, jnp.float32),
        "w_left": draw_w_left(jax.random.fold_in(arg_keys[12], 71), 0),
        "w_left_gate": draw_w_left_gate(jax.random.fold_in(arg_keys[12], 71), 0),
        "w_right": draw_w_right(jax.random.fold_in(arg_keys[12], 71), 0),
        "w_right_gate": draw_w_right_gate(jax.random.fold_in(arg_keys[12], 71), 0),
        "w_gate": noise(arg_keys[8], (C, C), C ** -0.5, 0.5),
        "ln_out_gain": jnp.clip(1.0 + 0.15 * jax.random.normal(arg_keys[9], (HID,), jnp.float32), 0.25, 1.75),
        "ln_out_bias": noise(arg_keys[10], (HID,), 0.5, 3.0, jnp.float32),
        "w_out": noise(arg_keys[11], (HID, C), HID ** -0.5, 0.5),
    }


def normalize(values, gain, bias):
    mean = lax.optimization_barrier(jnp.mean(values, axis=-1, keepdims=True))
    centred = values - mean
    variance = lax.optimization_barrier(jnp.mean(centred * centred, axis=-1, keepdims=True))
    return centred * jax.lax.rsqrt(variance + 1e-05) * gain + bias

def reference(pair, token_mask, ln_in_gain, ln_in_bias, w_left, w_left_gate, w_right, w_right_gate, w_gate, ln_out_gain, ln_out_bias, w_out):
    normed = normalize(pair.astype(jnp.float32), ln_in_gain, ln_in_bias).astype(jnp.bfloat16)
    flat = normed.reshape(TOKENS * TOKENS, C)
    maskf = token_mask.astype(jnp.float32)
    pair_mask = (maskf[:, None] * maskf[None, :]).reshape(TOKENS * TOKENS, 1)
    left_proj = jnp.dot(flat, w_left, preferred_element_type=jnp.float32)
    left_gate = jnp.dot(flat, w_left_gate, preferred_element_type=jnp.float32)
    left = (pair_mask * jax.nn.sigmoid(left_gate) * left_proj).astype(jnp.bfloat16)
    right_proj = jnp.dot(flat, w_right, preferred_element_type=jnp.float32)
    right_gate = jnp.dot(flat, w_right_gate, preferred_element_type=jnp.float32)
    right = (pair_mask * jax.nn.sigmoid(right_gate) * right_proj).astype(jnp.bfloat16)
    left_t = jnp.transpose(left.reshape(TOKENS, TOKENS, HID).astype(jnp.float32), (2, 0, 1))
    right_t = jnp.transpose(right.reshape(TOKENS, TOKENS, HID).astype(jnp.float32), (2, 0, 1))
    triangle = jnp.einsum('cik,cjk->cij', left_t, right_t)
    triangle = jnp.transpose(triangle, (1, 2, 0)).reshape(TOKENS * TOKENS, HID)
    triangle_normed = normalize(triangle, ln_out_gain, ln_out_bias).astype(jnp.bfloat16)
    gate = jax.nn.sigmoid(jnp.dot(flat, w_gate, preferred_element_type=jnp.float32))
    update = gate * jnp.dot(triangle_normed, w_out, preferred_element_type=jnp.float32)
    return update.astype(jnp.bfloat16).reshape(TOKENS, TOKENS, C)
```

```python
import jax
import jax.numpy as jnp
from jax import lax
from jax.experimental import pallas as pl
from jax.experimental.pallas import tpu as pltpu
from jax.sharding import Mesh, PartitionSpec as P

F32 = jnp.float32
BF16 = jnp.bfloat16
NT = (((1,), (1,)), ((), ()))
TN = (((0,), (0,)), ((), ()))
PARAMS = pltpu.CompilerParams(vmem_limit_bytes=24 * 1024 * 1024)
VMEM = pl.BlockSpec(memory_space=pltpu.VMEM)
SMEM = pl.BlockSpec(memory_space=pltpu.SMEM)


def low_lanes(shape):
    return lax.broadcasted_iota(jnp.int32, shape, len(shape) - 1) < 64


def project(
    mask_scalars, mask_rows, x_ref, gain, bias, w_l, w_lg, w_r, w_rg, out_ref, normed_ref, rows
):
    row, core = lax.axis_index("row"), lax.axis_index("core")
    x = x_ref[...].astype(F32)
    centred = x - jnp.mean(x, axis=-1, keepdims=True)
    variance = jnp.mean(centred * centred, axis=-1, keepdims=True)
    normed = (centred * lax.rsqrt(variance + 1e-05) * gain[...] + bias[...]).astype(BF16)
    normed_ref[...] = normed
    weights = jnp.concatenate([w[...].T for w in (w_l, w_lg, w_r, w_rg)], axis=0)
    mask_k = mask_rows[pl.ds(lax.axis_index("zl"), 1), :].astype(F32)
    swapped = pltpu.roll(mask_k, 64, 1)
    low = low_lanes((1, 128))
    mask_k = jnp.where(low == (core == 0), mask_k, swapped)
    for s in range(8):
        tokens = jnp.concatenate([normed[s], normed[s + 8]], axis=0)
        p = lax.dot_general(weights, tokens, NT, preferred_element_type=F32)
        mask_a = mask_scalars[row * 16 + s].astype(F32)
        mask_b = mask_scalars[row * 16 + s + 8].astype(F32)
        mask = mask_k * jnp.where(low, mask_a, mask_b)
        left = mask * jax.nn.sigmoid(p[128:256]) * p[:128]
        right = mask * jax.nn.sigmoid(p[384:]) * p[256:384]
        rows[pl.ds(s, 128, stride=16), :] = left
        rows[pl.ds(8 + s, 128, stride=16), :] = right
    out_ref[...] = rows[...].reshape(128, 16, 128).astype(BF16)


def contract(s_ref, keep_ref, send_ref):
    core = lax.axis_index("core")
    edges = s_ref[...].astype(F32).reshape(32, 4, 16, 128)
    low = low_lanes((256, 128))
    left_a, left_b, right, swapped = [], [], [], []
    for z in range(4):
        left_z = edges[:, z, :8].reshape(256, 128)
        right_z = edges[:, z, 8:].reshape(256, 128)
        left_a.append(jnp.where(low, left_z, 0.0).astype(BF16))
        left_b.append(jnp.where(low, 0.0, left_z).astype(BF16))
        right.append(right_z.astype(BF16))
        swapped.append(pltpu.roll(right_z, 64, 1).astype(BF16))
    left = jnp.concatenate(
        [jnp.concatenate(left_a, axis=1), jnp.concatenate(left_b, axis=1)], axis=0
    )
    right = jnp.concatenate(right, axis=1).reshape(4, 2, 32, 512)
    swapped = jnp.concatenate(swapped, axis=1).reshape(4, 2, 32, 512)
    both = jnp.concatenate([right, swapped], axis=2)
    first, second = both[:, 0].reshape(256, 512), both[:, 1].reshape(256, 512)
    mine = jnp.where(core == 0, first, second)
    other = jnp.where(core == 0, second, first)
    send_ref[...] = lax.dot_general(left, other, NT, preferred_element_type=F32)
    keep_ref[...] = lax.dot_general(left, mine, NT, preferred_element_type=F32)


def add_halves(keep_ref, got_ref, out_ref):
    low = low_lanes((256, 128))
    for v in range(2):
        cols = slice(128 * v, 128 * v + 128)
        a = keep_ref[:256, cols] + got_ref[:256, cols]
        b = keep_ref[256:, cols] + got_ref[256:, cols]
        even = jnp.where(low, a, pltpu.roll(b, 64, 1))
        odd = jnp.where(low, pltpu.roll(a, 64, 1), b)
        out_ref[:, 2 * v] = even.reshape(32, 8, 128).astype(BF16)
        out_ref[:, 2 * v + 1] = odd.reshape(32, 8, 128).astype(BF16)


def finish(t_ref, normed_ref, w_gate, gain, bias, w_out, out_ref, rows):
    t = t_ref[...].astype(F32)
    centred = t - jnp.mean(t, axis=0, keepdims=True)
    variance = jnp.mean(centred * centred, axis=0, keepdims=True)
    rows[...] = (centred * lax.rsqrt(variance + 1e-05)).reshape(1024, 128)
    gain_col = jnp.broadcast_to(gain[...], (128, 128)).T
    bias_col = jnp.broadcast_to(bias[...], (128, 128)).T
    w = w_out[...]
    for s in range(8):
        n = (rows[pl.ds(s, 128, stride=8), :] * gain_col + bias_col).astype(BF16)
        y = lax.dot_general(n, w, TN, preferred_element_type=F32).reshape(2, 2, 4, 8, 128)
        for b in range(2):
            i = s + 8 * b
            gate = jax.nn.sigmoid(
                jnp.dot(normed_ref[i], w_gate[...], preferred_element_type=F32)
            )
            token = jnp.stack([y[b, b], y[b, 1 - b]], axis=1).reshape(64, 128)
            out_ref[i] = (gate * token).astype(BF16)


def call(kernel, outs, specs, scratch=()):
    return pl.pallas_call(
        kernel,
        out_shape=outs,
        in_specs=specs,
        out_specs=jax.tree.map(lambda _: VMEM, outs),
        scratch_shapes=scratch,
        compiler_params=PARAMS,
    )


def shape(*dims, dtype=BF16):
    return jax.ShapeDtypeStruct(dims, dtype)


def shards(
    pair,
    token_mask,
    ln_in_gain,
    ln_in_bias,
    w_left,
    w_left_gate,
    w_right,
    w_right_gate,
    w_gate,
    ln_out_gain,
    ln_out_bias,
    w_out,
):
    edges, normed = call(
        project,
        (shape(128, 16, 128), shape(16, 64, 128)),
        [SMEM] + [VMEM] * 8,
        [pltpu.VMEM((2048, 128), F32)],
    )(
        token_mask,
        token_mask.reshape(4, 128),
        pair,
        ln_in_gain.reshape(1, 128),
        ln_in_bias.reshape(1, 128),
        w_left,
        w_left_gate,
        w_right,
        w_right_gate,
    )
    edges = lax.all_to_all(edges, ("row", "zl"), 0, 0, tiled=True)
    keep, send = call(
        contract, (shape(512, 256, dtype=F32), shape(512, 256, dtype=F32)), [VMEM]
    )(edges)
    got = lax.ppermute(send, "core", [(0, 1), (1, 0)])
    triangle = call(add_halves, shape(32, 4, 8, 128), [VMEM] * 2)(keep, got)
    triangle = lax.all_to_all(
        triangle.reshape(128, 8, 128), ("row", "zl"), 0, 0, tiled=True
    )
    return call(
        finish, shape(16, 64, 128), [VMEM] * 6, [pltpu.VMEM((1024, 128), F32)]
    )(
        triangle,
        normed,
        w_gate,
        ln_out_gain.reshape(1, 128),
        ln_out_bias.reshape(1, 128),
        w_out,
    )


def solution(mesh):
    fine = Mesh(mesh.devices.reshape(32, 4, 2), ("row", "zl", "core"))
    tile = P("row", ("zl", "core"), None)
    return jax.shard_map(
        shards, mesh=fine, in_specs=(tile,) + (P(),) * 11, out_specs=tile, check_vma=False
    )
```

```python
import jax
import jax.numpy as jnp
from jax import lax
from jax.experimental import pallas as pl
from jax.experimental.pallas import tpu as pltpu
from jax.sharding import Mesh, PartitionSpec as P

F32 = jnp.float32
BF16 = jnp.bfloat16
NT = (((1,), (1,)), ((), ()))
TN = (((0,), (0,)), ((), ()))
MIB = 1024 * 1024
VMEM = pl.BlockSpec(memory_space=pltpu.VMEM)
HBM = pl.BlockSpec(memory_space=pltpu.HBM)
PEERS = ("y", "zl", "zh", "x")


def low_lanes(shape):
    return lax.broadcasted_iota(jnp.int32, shape, len(shape) - 1) < 64


def fetch(sources, targets, sems):
    copies = [
        pltpu.make_async_copy(source, target, sems.at[n])
        for n, (source, target) in enumerate(zip(sources, targets))
    ]
    for copy in copies:
        copy.start()
    return copies


def project(
    x_hbm, mask_flat, mask_rows, gain_hbm, bias_hbm, w_l, w_lg, w_r, w_rg,
    out_ref, normed_ref,
    x_ref, mask_scalars, mask_ref, gain, bias, w_ref, rows, sems,
):
    copies = fetch(
        (x_hbm, gain_hbm, bias_hbm, mask_flat, mask_rows, w_l, w_lg, w_r, w_rg),
        (x_ref, gain, bias, mask_scalars, mask_ref) + tuple(w_ref.at[n] for n in range(4)),
        sems,
    )
    row = lax.axis_index("y") * 8 + lax.axis_index("zh") * 4 + lax.axis_index("x")
    core = lax.axis_index("core")
    copies[0].wait()
    x = x_ref[...].astype(F32)
    centred = x - jnp.mean(x, axis=-1, keepdims=True)
    variance = jnp.mean(centred * centred, axis=-1, keepdims=True)
    for copy in copies[1:]:
        copy.wait()
    normed = (centred * lax.rsqrt(variance + 1e-05) * gain[...] + bias[...]).astype(BF16)
    normed_ref[...] = normed
    weights = jnp.concatenate([w_ref[n].T for n in range(4)], axis=0)
    mask_k = mask_ref[pl.ds(lax.axis_index("zl"), 1), :].astype(F32)
    swapped = pltpu.roll(mask_k, 64, 1)
    low = low_lanes((1, 128))
    mask_k = jnp.where(low == (core == 0), mask_k, swapped)
    for s in range(8):
        tokens = jnp.concatenate([normed[s], normed[s + 8]], axis=0)
        p = lax.dot_general(weights, tokens, NT, preferred_element_type=F32)
        mask_a = mask_scalars[row * 16 + s].astype(F32)
        mask_b = mask_scalars[row * 16 + s + 8].astype(F32)
        mask = mask_k * jnp.where(low, mask_a, mask_b)
        left = mask * jax.nn.sigmoid(p[128:256]) * p[:128]
        right = mask * jax.nn.sigmoid(p[384:]) * p[256:384]
        rows[pl.ds(s, 128, stride=16), :] = left
        rows[pl.ds(8 + s, 128, stride=16), :] = right
    out_ref[...] = rows[...].reshape(128, 16, 128).astype(BF16)


def contract(s_ref, keep_ref, send_ref):
    core = lax.axis_index("core")
    edges = s_ref[...].astype(F32).reshape(4, 4, 8, 16, 128)
    low = low_lanes((256, 128))
    left_a, left_b, right, swapped = [], [], [], []
    for z in range(4):
        left_z = edges[:, z, :, :8].reshape(256, 128)
        right_z = edges[:, z, :, 8:].reshape(256, 128)
        left_a.append(jnp.where(low, left_z, 0.0).astype(BF16))
        left_b.append(jnp.where(low, 0.0, left_z).astype(BF16))
        right.append(right_z.astype(BF16))
        swapped.append(pltpu.roll(right_z, 64, 1).astype(BF16))
    left = jnp.concatenate(
        [jnp.concatenate(left_a, axis=1), jnp.concatenate(left_b, axis=1)], axis=0
    )
    right = jnp.concatenate(right, axis=1).reshape(4, 2, 32, 512)
    swapped = jnp.concatenate(swapped, axis=1).reshape(4, 2, 32, 512)
    both = jnp.concatenate([right, swapped], axis=2)
    first, second = both[:, 0].reshape(256, 512), both[:, 1].reshape(256, 512)
    mine = jnp.where(core == 0, first, second)
    other = jnp.where(core == 0, second, first)
    send_ref[...] = lax.dot_general(left, other, NT, preferred_element_type=F32).astype(BF16)
    keep_ref[...] = lax.dot_general(left, mine, NT, preferred_element_type=F32)


def prepare(
    normed_ref, w_gate, w_out_hbm, gain_hbm, bias_hbm,
    gate_ref, w_out_ref, affine_ref,
    w_ref, gain, bias, sems,
):
    copies = fetch(
        (w_gate, w_out_hbm, gain_hbm, bias_hbm), (w_ref, w_out_ref, gain, bias), sems
    )
    for copy in copies:
        copy.wait()
    flat = normed_ref[...].reshape(1024, 128)
    gate = jax.nn.sigmoid(jnp.dot(flat, w_ref[...], preferred_element_type=F32))
    gate_ref[...] = gate.reshape(16, 64, 128)
    affine_ref[0] = jnp.broadcast_to(gain[...], (128, 128)).T
    affine_ref[1] = jnp.broadcast_to(bias[...], (128, 128)).T


def add_halves(keep_ref, got_ref, out_ref):
    low = low_lanes((256, 128))
    for v in range(2):
        cols = slice(128 * v, 128 * v + 128)
        a = keep_ref[:256, cols] + got_ref[:256, cols].astype(F32)
        b = keep_ref[256:, cols] + got_ref[256:, cols].astype(F32)
        even = jnp.where(low, a, pltpu.roll(b, 64, 1))
        odd = jnp.where(low, pltpu.roll(a, 64, 1), b)
        out_ref[:, 2 * v] = even.reshape(4, 8, 8, 128).astype(BF16)
        out_ref[:, 2 * v + 1] = odd.reshape(4, 8, 8, 128).astype(BF16)


def finish(t_ref, gate_ref, w_out, affine, out_hbm, rows, out_ref, sems):
    t = t_ref[...].astype(F32)
    centred = t - jnp.mean(t, axis=0, keepdims=True)
    variance = jnp.mean(centred * centred, axis=0, keepdims=True)
    rows[...] = (centred * lax.rsqrt(variance + 1e-05)).reshape(1024, 128)
    gain_col, bias_col = affine[0], affine[1]
    w = w_out[...]
    copies = []
    for s in range(8):
        n = (rows[pl.ds(s, 128, stride=8), :] * gain_col + bias_col).astype(BF16)
        y = lax.dot_general(n, w, TN, preferred_element_type=F32).reshape(2, 2, 4, 8, 128)
        for b in range(2):
            i = s + 8 * b
            token = jnp.stack([y[b, b], y[b, 1 - b]], axis=1).reshape(64, 128)
            out_ref[i] = (gate_ref[i] * token).astype(BF16)
        if s % 4 == 3:
            for b in range(2):
                part = pl.ds(s - 3 + 8 * b, 4)
                copies.append(
                    pltpu.make_async_copy(
                        out_ref.at[part], out_hbm.at[part], sems.at[len(copies)]
                    )
                )
                copies[-1].start()
    for copy in copies:
        copy.wait()


def call(kernel, outs, specs, scratch=(), out_spec=VMEM, cost=None, limit=24):
    return pl.pallas_call(
        kernel,
        out_shape=outs,
        in_specs=specs,
        out_specs=jax.tree.map(lambda _: out_spec, outs),
        scratch_shapes=scratch,
        compiler_params=pltpu.CompilerParams(vmem_limit_bytes=limit * MIB),
        cost_estimate=cost,
    )


def shape(*dims, dtype=BF16):
    return jax.ShapeDtypeStruct(dims, dtype)


def shards(
    pair,
    token_mask,
    ln_in_gain,
    ln_in_bias,
    w_left,
    w_left_gate,
    w_right,
    w_right_gate,
    w_gate,
    ln_out_gain,
    ln_out_bias,
    w_out,
):
    edges, normed = call(
        project,
        (shape(128, 16, 128), shape(16, 64, 128)),
        [HBM] * 9,
        [
            pltpu.VMEM((16, 64, 128), BF16),
            pltpu.SMEM((512,), jnp.int32),
            pltpu.VMEM((4, 128), jnp.int32),
            pltpu.VMEM((1, 128), F32),
            pltpu.VMEM((1, 128), F32),
            pltpu.VMEM((4, 128, 128), BF16),
            pltpu.VMEM((2048, 128), F32),
            pltpu.SemaphoreType.DMA((9,)),
        ],
        limit=60,
    )(
        pair,
        token_mask,
        token_mask.reshape(4, 128),
        ln_in_gain.reshape(1, 128),
        ln_in_bias.reshape(1, 128),
        w_left,
        w_left_gate,
        w_right,
        w_right_gate,
    )
    edges = lax.all_to_all(edges, PEERS, 0, 0, tiled=True)
    keep, send = call(contract, (shape(512, 256, dtype=F32), shape(512, 256)), [VMEM])(edges)
    got = lax.ppermute(send, "core", [(0, 1), (1, 0)])
    normed, keep = lax.optimization_barrier((normed, keep))
    gate, w_out, affine = call(
        prepare,
        (shape(16, 64, 128, dtype=F32), shape(128, 128), shape(2, 128, 128, dtype=F32)),
        [VMEM] + [HBM] * 4,
        [
            pltpu.VMEM((128, 128), BF16),
            pltpu.VMEM((1, 128), F32),
            pltpu.VMEM((1, 128), F32),
            pltpu.SemaphoreType.DMA((4,)),
        ],
        cost=pl.CostEstimate(
            flops=2 * 1024 * 128 * 128, bytes_accessed=1 << 20, transcendentals=1 << 18
        ),
    )(normed, w_gate, w_out, ln_out_gain.reshape(1, 128), ln_out_bias.reshape(1, 128))
    gate, keep = lax.optimization_barrier((gate, keep))
    triangle = call(add_halves, shape(4, 4, 8, 8, 128), [VMEM] * 2)(keep, got)
    triangle = lax.all_to_all(triangle.reshape(128, 8, 128), PEERS, 0, 0, tiled=True)
    return call(
        finish,
        shape(16, 64, 128),
        [VMEM] * 4,
        [
            pltpu.VMEM((1024, 128), F32),
            pltpu.VMEM((16, 64, 128), BF16),
            pltpu.SemaphoreType.DMA((4,)),
        ],
        out_spec=HBM,
    )(triangle, gate, w_out, affine)


def solution(mesh):
    fine = Mesh(mesh.devices.reshape(4, 2, 4, 4, 2), ("y", "zh", "x", "zl", "core"))
    tile = P(("y", "zh", "x"), ("zl", "core"), None)
    return jax.shard_map(
        shards, mesh=fine, in_specs=(tile,) + (P(),) * 11, out_specs=tile, check_vma=False
    )
```

```python
import jax
import jax.numpy as jnp
from jax import lax
from jax.experimental import pallas as pl
from jax.experimental.pallas import tpu as pltpu
from jax.sharding import Mesh, PartitionSpec as P

F32 = jnp.float32
BF16 = jnp.bfloat16
NT = (((1,), (1,)), ((), ()))
TN = (((0,), (0,)), ((), ()))
MIB = 1024 * 1024
VMEM = pl.BlockSpec(memory_space=pltpu.VMEM)
HBM = pl.BlockSpec(memory_space=pltpu.HBM)
PEERS = ("zl", "zh", "y", "x")


def low_lanes(shape):
    return lax.broadcasted_iota(jnp.int32, shape, len(shape) - 1) < 64


def fetch(sources, targets, sems):
    copies = [
        pltpu.make_async_copy(source, target, sems.at[n])
        for n, (source, target) in enumerate(zip(sources, targets))
    ]
    for copy in copies:
        copy.start()
    return copies


def project(
    x_hbm, mask_flat, mask_rows, gain_hbm, bias_hbm, w_l, w_lg, w_r, w_rg,
    out_ref, normed_ref,
    x_ref, mask_scalars, mask_ref, gain, bias, w_ref, rows, sems,
):
    copies = fetch(
        (x_hbm, gain_hbm, bias_hbm, mask_flat, mask_rows, w_l, w_lg, w_r, w_rg),
        (x_ref, gain, bias, mask_scalars, mask_ref) + tuple(w_ref.at[n] for n in range(4)),
        sems,
    )
    row = lax.axis_index("y") * 8 + lax.axis_index("zh") * 4 + lax.axis_index("x")
    core = lax.axis_index("core")
    copies[0].wait()
    x = x_ref[...].astype(F32)
    centred = x - jnp.mean(x, axis=-1, keepdims=True)
    variance = jnp.mean(centred * centred, axis=-1, keepdims=True)
    for copy in copies[1:]:
        copy.wait()
    normed = (centred * lax.rsqrt(variance + 1e-05) * gain[...] + bias[...]).astype(BF16)
    normed_ref[...] = normed
    weights = jnp.concatenate([w_ref[n].T for n in range(4)], axis=0)
    mask_k = mask_ref[pl.ds(lax.axis_index("zl"), 1), :].astype(F32)
    swapped = pltpu.roll(mask_k, 64, 1)
    low = low_lanes((1, 128))
    mask_k = jnp.where(low == (core == 0), mask_k, swapped)
    for s in range(8):
        tokens = jnp.concatenate([normed[s], normed[s + 8]], axis=0)
        p = lax.dot_general(weights, tokens, NT, preferred_element_type=F32)
        mask_a = mask_scalars[row * 16 + s].astype(F32)
        mask_b = mask_scalars[row * 16 + s + 8].astype(F32)
        mask = mask_k * jnp.where(low, mask_a, mask_b)
        left = mask * jax.nn.sigmoid(p[128:256]) * p[:128]
        right = mask * jax.nn.sigmoid(p[384:]) * p[256:384]
        rows[pl.ds(s, 128, stride=16), :] = left
        rows[pl.ds(8 + s, 128, stride=16), :] = right
    out_ref[...] = rows[...].reshape(128, 16, 128).astype(BF16)


def contract(s_ref, keep_ref, send_ref):
    core = lax.axis_index("core")
    edges = s_ref[...].astype(F32).reshape(4, 2, 4, 4, 16, 128)
    edges = jnp.stack([edges[:, 0], edges[:, 1]], axis=2).reshape(4, 32, 16, 128)
    low = low_lanes((256, 128))
    left_a, left_b, right, swapped = [], [], [], []
    for z in range(4):
        left_z = edges[z, :, :8].reshape(256, 128)
        right_z = edges[z, :, 8:].reshape(256, 128)
        left_a.append(jnp.where(low, left_z, 0.0).astype(BF16))
        left_b.append(jnp.where(low, 0.0, left_z).astype(BF16))
        right.append(right_z.astype(BF16))
        swapped.append(pltpu.roll(right_z, 64, 1).astype(BF16))
    left = jnp.concatenate(
        [jnp.concatenate(left_a, axis=1), jnp.concatenate(left_b, axis=1)], axis=0
    )
    right = jnp.concatenate(right, axis=1).reshape(4, 2, 32, 512)
    swapped = jnp.concatenate(swapped, axis=1).reshape(4, 2, 32, 512)
    both = jnp.concatenate([right, swapped], axis=2)
    first, second = both[:, 0].reshape(256, 512), both[:, 1].reshape(256, 512)
    mine = jnp.where(core == 0, first, second)
    other = jnp.where(core == 0, second, first)
    send_ref[...] = lax.dot_general(left, other, NT, preferred_element_type=F32).astype(BF16)
    keep_ref[...] = lax.dot_general(left, mine, NT, preferred_element_type=F32)


def prepare(
    normed_ref, w_gate, w_out_hbm, gain_hbm, bias_hbm,
    gate_ref, w_out_ref, affine_ref,
    w_ref, gain, bias, sems,
):
    copies = fetch(
        (w_gate, w_out_hbm, gain_hbm, bias_hbm), (w_ref, w_out_ref, gain, bias), sems
    )
    for copy in copies:
        copy.wait()
    flat = normed_ref[...].reshape(1024, 128)
    gate = jax.nn.sigmoid(jnp.dot(flat, w_ref[...], preferred_element_type=F32))
    gate_ref[...] = gate.reshape(16, 64, 128)
    affine_ref[0] = jnp.broadcast_to(gain[...], (128, 128)).T
    affine_ref[1] = jnp.broadcast_to(bias[...], (128, 128)).T


def add_halves(keep_ref, got_ref, out_ref):
    low = low_lanes((256, 128))
    for v in range(2):
        cols = slice(128 * v, 128 * v + 128)
        a = keep_ref[:256, cols] + got_ref[:256, cols].astype(F32)
        b = keep_ref[256:, cols] + got_ref[256:, cols].astype(F32)
        even = jnp.where(low, a, pltpu.roll(b, 64, 1))
        odd = jnp.where(low, pltpu.roll(a, 64, 1), b)
        even = even.reshape(4, 2, 4, 8, 128).astype(BF16)
        odd = odd.reshape(4, 2, 4, 8, 128).astype(BF16)
        for zh in range(2):
            out_ref[2 * v, zh] = even[:, zh]
            out_ref[2 * v + 1, zh] = odd[:, zh]


def finish(t_ref, gate_ref, w_out, affine, out_hbm, rows, out_ref, sems):
    t = t_ref[...].astype(F32)
    centred = t - jnp.mean(t, axis=0, keepdims=True)
    variance = jnp.mean(centred * centred, axis=0, keepdims=True)
    rows[...] = (centred * lax.rsqrt(variance + 1e-05)).reshape(1024, 128)
    gain_col, bias_col = affine[0], affine[1]
    w = w_out[...]
    copies = []
    for s in range(8):
        n = (rows[pl.ds(s, 128, stride=8), :] * gain_col + bias_col).astype(BF16)
        y = lax.dot_general(n, w, TN, preferred_element_type=F32).reshape(2, 2, 4, 8, 128)
        for b in range(2):
            i = s + 8 * b
            token = jnp.stack([y[b, b], y[b, 1 - b]], axis=1).reshape(64, 128)
            out_ref[i] = (gate_ref[i] * token).astype(BF16)
        if s % 4 == 3:
            for b in range(2):
                part = pl.ds(s - 3 + 8 * b, 4)
                copies.append(
                    pltpu.make_async_copy(
                        out_ref.at[part], out_hbm.at[part], sems.at[len(copies)]
                    )
                )
                copies[-1].start()
    for copy in copies:
        copy.wait()


def call(kernel, outs, specs, scratch=(), out_spec=VMEM, cost=None, limit=24):
    return pl.pallas_call(
        kernel,
        out_shape=outs,
        in_specs=specs,
        out_specs=jax.tree.map(lambda _: out_spec, outs),
        scratch_shapes=scratch,
        compiler_params=pltpu.CompilerParams(vmem_limit_bytes=limit * MIB),
        cost_estimate=cost,
    )


def in_hbm(*arrays):
    return [pltpu.with_memory_space_constraint(a, pltpu.HBM) for a in arrays]


def shape(*dims, dtype=BF16):
    return jax.ShapeDtypeStruct(dims, dtype)


def shards(
    pair,
    token_mask,
    ln_in_gain,
    ln_in_bias,
    w_left,
    w_left_gate,
    w_right,
    w_right_gate,
    w_gate,
    ln_out_gain,
    ln_out_bias,
    w_out,
):
    edges, normed = call(
        project,
        (shape(128, 16, 128), shape(16, 64, 128)),
        [HBM] * 9,
        [
            pltpu.VMEM((16, 64, 128), BF16),
            pltpu.SMEM((512,), jnp.int32),
            pltpu.VMEM((4, 128), jnp.int32),
            pltpu.VMEM((1, 128), F32),
            pltpu.VMEM((1, 128), F32),
            pltpu.VMEM((4, 128, 128), BF16),
            pltpu.VMEM((2048, 128), F32),
            pltpu.SemaphoreType.DMA((9,)),
        ],
    )(
        *in_hbm(
            pair,
            token_mask,
            token_mask.reshape(4, 128),
            ln_in_gain.reshape(1, 128),
            ln_in_bias.reshape(1, 128),
            w_left,
            w_left_gate,
            w_right,
            w_right_gate,
        )
    )
    edges = lax.all_to_all(edges, PEERS, 0, 0, tiled=True)
    keep, send = call(contract, (shape(512, 256, dtype=F32), shape(512, 256)), [VMEM])(edges)
    got = lax.ppermute(send, "core", [(0, 1), (1, 0)])
    normed, keep = lax.optimization_barrier((normed, keep))
    gate, w_out, affine = call(
        prepare,
        (shape(16, 64, 128, dtype=F32), shape(128, 128), shape(2, 128, 128, dtype=F32)),
        [VMEM] + [HBM] * 4,
        [
            pltpu.VMEM((128, 128), BF16),
            pltpu.VMEM((1, 128), F32),
            pltpu.VMEM((1, 128), F32),
            pltpu.SemaphoreType.DMA((4,)),
        ],
        cost=pl.CostEstimate(
            flops=2 * 1024 * 128 * 128, bytes_accessed=1 << 20, transcendentals=1 << 18
        ),
    )(
        normed,
        *in_hbm(w_gate, w_out, ln_out_gain.reshape(1, 128), ln_out_bias.reshape(1, 128)),
    )
    gate, keep = lax.optimization_barrier((gate, keep))
    triangle = call(add_halves, shape(4, 2, 4, 4, 8, 128), [VMEM] * 2)(keep, got)
    triangle = lax.all_to_all(triangle.reshape(128, 8, 128), PEERS, 0, 0, tiled=True)
    return call(
        finish,
        shape(16, 64, 128),
        [VMEM] * 4,
        [
            pltpu.VMEM((1024, 128), F32),
            pltpu.VMEM((16, 64, 128), BF16),
            pltpu.SemaphoreType.DMA((4,)),
        ],
        out_spec=HBM,
    )(triangle, gate, w_out, affine)


def solution(mesh):
    fine = Mesh(mesh.devices.reshape(4, 2, 4, 4, 2), ("y", "zh", "x", "zl", "core"))
    tile = P(("y", "zh", "x"), ("zl", "core"), None)
    return jax.shard_map(
        shards, mesh=fine, in_specs=(tile,) + (P(),) * 11, out_specs=tile, check_vma=False
    )
```

```python
import jax
import jax.numpy as jnp
from jax import lax
from jax.experimental import pallas as pl
from jax.experimental.pallas import tpu as pltpu
from jax.sharding import Mesh, PartitionSpec as P

F32 = jnp.float32
BF16 = jnp.bfloat16
NT = (((1,), (1,)), ((), ()))
TN = (((0,), (0,)), ((), ()))
MIB = 1024 * 1024
VMEM = pl.BlockSpec(memory_space=pltpu.VMEM)
HBM = pl.BlockSpec(memory_space=pltpu.HBM)
PEERS = ("zl", "zh", "y", "x")


def low_lanes(shape):
    return lax.broadcasted_iota(jnp.int32, shape, len(shape) - 1) < 64


def fetch(sources, targets, sems):
    copies = [
        pltpu.make_async_copy(source, target, sems.at[n])
        for n, (source, target) in enumerate(zip(sources, targets))
    ]
    for copy in copies:
        copy.start()
    return copies


def project(
    x_hbm, mask_flat, mask_rows, gain_hbm, bias_hbm, w_l, w_lg, w_r, w_rg,
    out_ref, normed_ref,
    x_ref, mask_scalars, mask_ref, gain, bias, w_ref, rows, sems,
):
    copies = fetch(
        (x_hbm, gain_hbm, bias_hbm, mask_flat, mask_rows, w_l, w_lg, w_r, w_rg),
        (x_ref, gain, bias, mask_scalars, mask_ref) + tuple(w_ref.at[n] for n in range(4)),
        sems,
    )
    row = lax.axis_index("y") * 8 + lax.axis_index("zh") * 4 + lax.axis_index("x")
    core = lax.axis_index("core")
    copies[0].wait()
    x = x_ref[...].astype(F32)
    centred = x - jnp.mean(x, axis=-1, keepdims=True)
    variance = jnp.mean(centred * centred, axis=-1, keepdims=True)
    for copy in copies[1:]:
        copy.wait()
    normed = (centred * lax.rsqrt(variance + 1e-05) * gain[...] + bias[...]).astype(BF16)
    normed_ref[...] = normed
    weights = jnp.concatenate([w_ref[n].T for n in range(4)], axis=0)
    mask_k = mask_ref[pl.ds(lax.axis_index("zl"), 1), :].astype(F32)
    swapped = pltpu.roll(mask_k, 64, 1)
    low = low_lanes((1, 128))
    mask_k = jnp.where(low == (core == 0), mask_k, swapped)
    pall = lax.dot_general(weights, jnp.concatenate([normed[(s//2)+8*(s%2)] for s in range(16)],axis=0), NT, preferred_element_type=F32)
    for s in range(8):
        p = pall[:, 128*s:128*s+128]
        mask_a = mask_scalars[row * 16 + s].astype(F32)
        mask_b = mask_scalars[row * 16 + s + 8].astype(F32)
        mask = mask_k * jnp.where(low, mask_a, mask_b)
        left = mask * jax.nn.sigmoid(p[128:256]) * p[:128]
        right = mask * jax.nn.sigmoid(p[384:]) * p[256:384]
        rows[pl.ds(s, 128, stride=8), :] = left
        rows[pl.ds(1024 + s, 128, stride=8), :] = right
    out_ref[...] = jnp.concatenate([rows[:1024].reshape(128,8,128), rows[1024:].reshape(128,8,128)],axis=1).astype(BF16)


def contract(s_ref, keep_ref, send_ref):
    core = lax.axis_index("core")
    edges = s_ref[...].astype(F32).reshape(4, 2, 4, 4, 16, 128)
    edges = jnp.stack([edges[:, 0], edges[:, 1]], axis=2).reshape(4, 32, 16, 128)
    low = low_lanes((256, 128))
    def halves(part):
        first, second = [], []
        for z in (0, 2):
            a, b = part(z), part(z + 1)
            first.append(jnp.where(low, a, pltpu.roll(b, 64, 1)).astype(BF16))
            second.append(jnp.where(low, pltpu.roll(a, 64, 1), b).astype(BF16))
        return jnp.concatenate(first, axis=1), jnp.concatenate(second, axis=1)

    left = jnp.concatenate(halves(lambda z: edges[z, :, :8].reshape(256, 128)), axis=0)
    right = halves(lambda z: edges[z, :, 8:].reshape(256, 128))
    both = jnp.concatenate([r.reshape(4, 2, 32, 256) for r in right], axis=2)
    first, second = both[:, 0].reshape(256, 256), both[:, 1].reshape(256, 256)
    mine = jnp.where(core == 0, first, second)
    other = jnp.where(core == 0, second, first)
    send_ref[...] = lax.dot_general(left, other, NT, preferred_element_type=F32).astype(BF16)
    keep_ref[...] = lax.dot_general(left, mine, NT, preferred_element_type=F32)


def prepare(
    normed_ref, w_gate, w_out_hbm, gain_hbm, bias_hbm,
    gate_ref, w_out_ref, affine_ref,
    w_ref, gain, bias, sems,
):
    copies = fetch(
        (w_gate, w_out_hbm, gain_hbm, bias_hbm), (w_ref, w_out_ref, gain, bias), sems
    )
    for copy in copies:
        copy.wait()
    flat = normed_ref[...].reshape(1024, 128)
    gate = jax.nn.sigmoid(jnp.dot(flat, w_ref[...], preferred_element_type=F32))
    gate_ref[...] = gate.reshape(16, 64, 128)
    affine_ref[0] = jnp.broadcast_to(gain[...], (128, 128)).T
    affine_ref[1] = jnp.broadcast_to(bias[...], (128, 128)).T


def add_halves(keep_ref, got_ref, out_ref):
    low = low_lanes((256, 128))
    for v in range(2):
        cols = slice(128 * v, 128 * v + 128)
        a = keep_ref[:256, cols] + got_ref[:256, cols].astype(F32)
        b = keep_ref[256:, cols] + got_ref[256:, cols].astype(F32)
        even = jnp.where(low, a, pltpu.roll(b, 64, 1))
        odd = jnp.where(low, pltpu.roll(a, 64, 1), b)
        even = even.reshape(4, 2, 4, 8, 128).astype(BF16)
        odd = odd.reshape(4, 2, 4, 8, 128).astype(BF16)
        for zh in range(2):
            out_ref[2 * v, zh] = even[:, zh]
            out_ref[2 * v + 1, zh] = odd[:, zh]


def finish(t_ref, gate_ref, w_out, affine, out_hbm, rows, out_ref, sems):
    t = t_ref[...].astype(F32)
    centred = t - jnp.mean(t, axis=0, keepdims=True)
    variance = jnp.mean(centred * centred, axis=0, keepdims=True)
    rows[...] = (centred * lax.rsqrt(variance + 1e-05)).reshape(1024, 128)
    gain_col, bias_col = affine[0], affine[1]
    w = w_out[...]
    copies = []
    for s in range(8):
        n = (rows[pl.ds(s, 128, stride=8), :] * gain_col + bias_col).astype(BF16)
        y = lax.dot_general(n, w, TN, preferred_element_type=F32).reshape(2, 2, 4, 8, 128)
        for b in range(2):
            i = s + 8 * b
            token = jnp.stack([y[b, 0], y[b, 1]], axis=1).reshape(64, 128)
            out_ref[i] = (gate_ref[i] * token).astype(BF16)
        if s % 4 == 3:
            for b in range(2):
                part = pl.ds(s - 3 + 8 * b, 4)
                copies.append(
                    pltpu.make_async_copy(
                        out_ref.at[part], out_hbm.at[part], sems.at[len(copies)]
                    )
                )
                copies[-1].start()
    for copy in copies:
        copy.wait()


def call(kernel, outs, specs, scratch=(), out_spec=VMEM, cost=None, limit=24):
    return pl.pallas_call(
        kernel,
        out_shape=outs,
        in_specs=specs,
        out_specs=jax.tree.map(lambda _: out_spec, outs),
        scratch_shapes=scratch,
        compiler_params=pltpu.CompilerParams(vmem_limit_bytes=limit * MIB),
        cost_estimate=cost,
    )


def in_hbm(*arrays):
    return [pltpu.with_memory_space_constraint(a, pltpu.HBM) for a in arrays]


def shape(*dims, dtype=BF16):
    return jax.ShapeDtypeStruct(dims, dtype)


def shards(
    pair,
    token_mask,
    ln_in_gain,
    ln_in_bias,
    w_left,
    w_left_gate,
    w_right,
    w_right_gate,
    w_gate,
    ln_out_gain,
    ln_out_bias,
    w_out,
):
    edges, normed = call(
        project,
        (shape(128, 16, 128), shape(16, 64, 128)),
        [HBM] * 9,
        [
            pltpu.VMEM((16, 64, 128), BF16),
            pltpu.SMEM((512,), jnp.int32),
            pltpu.VMEM((4, 128), jnp.int32),
            pltpu.VMEM((1, 128), F32),
            pltpu.VMEM((1, 128), F32),
            pltpu.VMEM((4, 128, 128), BF16),
            pltpu.VMEM((2048, 128), F32),
            pltpu.SemaphoreType.DMA((9,)),
        ],
    )(
        *in_hbm(
            pair,
            token_mask,
            token_mask.reshape(4, 128),
            ln_in_gain.reshape(1, 128),
            ln_in_bias.reshape(1, 128),
            w_left,
            w_left_gate,
            w_right,
            w_right_gate,
        )
    )
    edges = lax.all_to_all(edges, PEERS, 0, 0, tiled=True)
    keep, send = call(contract, (shape(512, 256, dtype=F32), shape(512, 256)), [VMEM])(edges)
    got = lax.ppermute(send, "core", [(0, 1), (1, 0)])
    normed, keep = lax.optimization_barrier((normed, keep))
    gate, w_out, affine = call(
        prepare,
        (shape(16, 64, 128, dtype=F32), shape(128, 128), shape(2, 128, 128, dtype=F32)),
        [VMEM] + [HBM] * 4,
        [
            pltpu.VMEM((128, 128), BF16),
            pltpu.VMEM((1, 128), F32),
            pltpu.VMEM((1, 128), F32),
            pltpu.SemaphoreType.DMA((4,)),
        ],
        cost=pl.CostEstimate(
            flops=2 * 1024 * 128 * 128, bytes_accessed=1 << 20, transcendentals=1 << 18
        ),
    )(
        normed,
        *in_hbm(w_gate, w_out, ln_out_gain.reshape(1, 128), ln_out_bias.reshape(1, 128)),
    )
    gate, keep = lax.optimization_barrier((gate, keep))
    triangle = call(add_halves, shape(4, 2, 4, 4, 8, 128), [VMEM] * 2)(keep, got)
    triangle = lax.all_to_all(triangle.reshape(128, 8, 128), PEERS, 0, 0, tiled=True)
    return call(
        finish,
        shape(16, 64, 128),
        [VMEM] * 4,
        [
            pltpu.VMEM((1024, 128), F32),
            pltpu.VMEM((16, 64, 128), BF16),
            pltpu.SemaphoreType.DMA((4,)),
        ],
        out_spec=HBM,
    )(triangle, gate, w_out, affine)


def solution(mesh):
    fine = Mesh(mesh.devices.reshape(4, 2, 4, 4, 2), ("y", "zh", "x", "zl", "core"))
    tile = P(("y", "zh", "x"), ("zl", "core"), None)
    return jax.shard_map(
        shards, mesh=fine, in_specs=(tile,) + (P(),) * 11, out_specs=tile, check_vma=False
    )
```

```python
import jax
import jax.numpy as jnp
from jax import lax
from jax.experimental import pallas as pl
from jax.experimental.pallas import tpu as pltpu
from jax.sharding import Mesh, PartitionSpec as P

F32 = jnp.float32
BF16 = jnp.bfloat16
NT = (((1,), (1,)), ((), ()))
TN = (((0,), (0,)), ((), ()))
MIB = 1024 * 1024
VMEM = pl.BlockSpec(memory_space=pltpu.VMEM)
HBM = pl.BlockSpec(memory_space=pltpu.HBM)
PEERS = ("zl", "zh", "y", "x")


def low_lanes(shape):
    return lax.broadcasted_iota(jnp.int32, shape, len(shape) - 1) < 64


def fetch(sources, targets, sems):
    copies = [
        pltpu.make_async_copy(source, target, sems.at[n])
        for n, (source, target) in enumerate(zip(sources, targets))
    ]
    for copy in copies:
        copy.start()
    return copies


def project(
    x_hbm, mask_flat, mask_rows, gain_hbm, bias_hbm, w_l, w_lg, w_r, w_rg,
    out_ref, normed_ref,
    x_ref, mask_scalars, mask_ref, gain, bias, w_ref, rows, sems,
):
    copies = fetch(
        (x_hbm, gain_hbm, bias_hbm, mask_flat, mask_rows, w_l, w_lg, w_r, w_rg),
        (x_ref, gain, bias, mask_scalars, mask_ref) + tuple(w_ref.at[n] for n in range(4)),
        sems,
    )
    row = lax.axis_index("y") * 8 + lax.axis_index("zh") * 4 + lax.axis_index("x")
    core = lax.axis_index("core")
    for copy in copies:
        copy.wait()
    weights = jnp.concatenate([w_ref[n].T for n in range(4)], axis=0)
    mask_k = mask_ref[pl.ds(lax.axis_index("zl"), 1), :].astype(F32)
    swapped = pltpu.roll(mask_k, 64, 1)
    low = low_lanes((1, 128))
    mask_k = jnp.where(low == (core == 0), mask_k, swapped)
    for first in range(0, 8, 2):
        parts = []
        for start in (first, first + 8):
            x = x_ref[start : start + 2].astype(F32)
            centred = x - jnp.mean(x, axis=-1, keepdims=True)
            variance = jnp.mean(centred * centred, axis=-1, keepdims=True)
            part = centred * lax.rsqrt(variance + 1e-05) * gain[...] + bias[...]
            parts.append(part.astype(BF16))
            normed_ref[start : start + 2] = parts[-1]
        tokens = jnp.stack(parts, axis=1).reshape(128 * 2, 128)
        projected = lax.dot_general(weights, tokens, NT, preferred_element_type=F32)
        for n in range(2):
            s = first + n
            p = projected[:, 128 * n : 128 * n + 128]
            mask_a = mask_scalars[row * 16 + s].astype(F32)
            mask_b = mask_scalars[row * 16 + s + 8].astype(F32)
            mask = mask_k * jnp.where(low, mask_a, mask_b)
            left = mask * jax.nn.sigmoid(p[128:256]) * p[:128]
            right = mask * jax.nn.sigmoid(p[384:]) * p[256:384]
            rows[pl.ds(s, 128, stride=8), :] = left
            rows[pl.ds(1024 + s, 128, stride=8), :] = right
    out_ref[...] = jnp.concatenate([rows[:1024].reshape(128,8,128), rows[1024:].reshape(128,8,128)],axis=1).astype(BF16)


def contract(s_ref, keep_ref, send_ref):
    core = lax.axis_index("core")
    edges = s_ref[...].astype(F32).reshape(4, 2, 4, 4, 16, 128)
    edges = jnp.stack([edges[:, 0], edges[:, 1]], axis=2).reshape(4, 32, 16, 128)
    low = low_lanes((256, 128))
    def halves(part):
        first, second = [], []
        for z in (0, 2):
            a, b = part(z), part(z + 1)
            first.append(jnp.where(low, a, pltpu.roll(b, 64, 1)).astype(BF16))
            second.append(jnp.where(low, pltpu.roll(a, 64, 1), b).astype(BF16))
        return jnp.concatenate(first, axis=1), jnp.concatenate(second, axis=1)

    left = jnp.concatenate(halves(lambda z: edges[z, :, :8].reshape(256, 128)), axis=0)
    right = halves(lambda z: edges[z, :, 8:].reshape(256, 128))
    both = jnp.concatenate([r.reshape(4, 2, 32, 256) for r in right], axis=2)
    first, second = both[:, 0].reshape(256, 256), both[:, 1].reshape(256, 256)
    mine = jnp.where(core == 0, first, second)
    other = jnp.where(core == 0, second, first)
    send_ref[...] = lax.dot_general(left, other, NT, preferred_element_type=F32).astype(BF16)
    keep_ref[...] = lax.dot_general(left, mine, NT, preferred_element_type=F32)


def prepare(
    normed_ref, w_gate, w_out_hbm, gain_hbm, bias_hbm,
    gate_ref, w_out_ref, affine_ref,
    w_ref, gain, bias, sems,
):
    copies = fetch(
        (w_gate, w_out_hbm, gain_hbm, bias_hbm), (w_ref, w_out_ref, gain, bias), sems
    )
    for copy in copies:
        copy.wait()
    flat = normed_ref[...].reshape(1024, 128)
    gate = jax.nn.sigmoid(jnp.dot(flat, w_ref[...], preferred_element_type=F32))
    gate_ref[...] = gate.reshape(16, 64, 128)
    affine_ref[0] = jnp.broadcast_to(gain[...], (128, 128)).T
    affine_ref[1] = jnp.broadcast_to(bias[...], (128, 128)).T


def add_halves(keep_ref, got_ref, out_ref):
    low = low_lanes((256, 128))
    for v in range(2):
        cols = slice(128 * v, 128 * v + 128)
        a = keep_ref[:256, cols] + got_ref[:256, cols].astype(F32)
        b = keep_ref[256:, cols] + got_ref[256:, cols].astype(F32)
        even = jnp.where(low, a, pltpu.roll(b, 64, 1))
        odd = jnp.where(low, pltpu.roll(a, 64, 1), b)
        even = even.reshape(4, 2, 4, 8, 128).astype(BF16)
        odd = odd.reshape(4, 2, 4, 8, 128).astype(BF16)
        for zh in range(2):
            out_ref[2 * v, zh] = even[:, zh]
            out_ref[2 * v + 1, zh] = odd[:, zh]


def finish(t_ref, gate_ref, w_out, affine, out_hbm, rows, out_ref, sems):
    t = t_ref[...].astype(F32)
    rows[...] = t.reshape(1024, 128)
    gain_col, bias_col = affine[0], affine[1]
    w = w_out[...]
    copies = []
    for s in range(8):
        n = rows[pl.ds(s, 128, stride=8), :]
        n = n - jnp.mean(n, axis=0, keepdims=True)
        variance = jnp.mean(n * n, axis=0, keepdims=True)
        n = (n * lax.rsqrt(variance + 1e-05) * gain_col + bias_col).astype(BF16)
        y = lax.dot_general(n, w, TN, preferred_element_type=F32).reshape(2, 2, 4, 8, 128)
        for b in range(2):
            i = s + 8 * b
            token = jnp.stack([y[b, 0], y[b, 1]], axis=1).reshape(64, 128)
            out_ref[i] = (gate_ref[i] * token).astype(BF16)
        if s % 4 == 3:
            for b in range(2):
                part = pl.ds(s - 3 + 8 * b, 4)
                copies.append(
                    pltpu.make_async_copy(
                        out_ref.at[part], out_hbm.at[part], sems.at[len(copies)]
                    )
                )
                copies[-1].start()
    for copy in copies:
        copy.wait()


def call(kernel, outs, specs, scratch=(), out_spec=VMEM, cost=None, limit=24):
    return pl.pallas_call(
        kernel,
        out_shape=outs,
        in_specs=specs,
        out_specs=jax.tree.map(lambda _: out_spec, outs),
        scratch_shapes=scratch,
        compiler_params=pltpu.CompilerParams(vmem_limit_bytes=limit * MIB),
        cost_estimate=cost,
    )


def in_hbm(*arrays):
    return [pltpu.with_memory_space_constraint(a, pltpu.HBM) for a in arrays]


def shape(*dims, dtype=BF16):
    return jax.ShapeDtypeStruct(dims, dtype)


def shards(
    pair,
    token_mask,
    ln_in_gain,
    ln_in_bias,
    w_left,
    w_left_gate,
    w_right,
    w_right_gate,
    w_gate,
    ln_out_gain,
    ln_out_bias,
    w_out,
):
    edges, normed = call(
        project,
        (shape(128, 16, 128), shape(16, 64, 128)),
        [HBM] * 9,
        [
            pltpu.VMEM((16, 64, 128), BF16),
            pltpu.SMEM((512,), jnp.int32),
            pltpu.VMEM((4, 128), jnp.int32),
            pltpu.VMEM((1, 128), F32),
            pltpu.VMEM((1, 128), F32),
            pltpu.VMEM((4, 128, 128), BF16),
            pltpu.VMEM((2048, 128), F32),
            pltpu.SemaphoreType.DMA((9,)),
        ],
    )(
        *in_hbm(
            pair,
            token_mask,
            token_mask.reshape(4, 128),
            ln_in_gain.reshape(1, 128),
            ln_in_bias.reshape(1, 128),
            w_left,
            w_left_gate,
            w_right,
            w_right_gate,
        )
    )
    edges = lax.all_to_all(edges, PEERS, 0, 0, tiled=True)
    keep, send = call(contract, (shape(512, 256, dtype=F32), shape(512, 256)), [VMEM])(edges)
    got = lax.ppermute(send, "core", [(0, 1), (1, 0)])
    normed, keep = lax.optimization_barrier((normed, keep))
    gate, w_out, affine = call(
        prepare,
        (shape(16, 64, 128, dtype=F32), shape(128, 128), shape(2, 128, 128, dtype=F32)),
        [VMEM] + [HBM] * 4,
        [
            pltpu.VMEM((128, 128), BF16),
            pltpu.VMEM((1, 128), F32),
            pltpu.VMEM((1, 128), F32),
            pltpu.SemaphoreType.DMA((4,)),
        ],
        cost=pl.CostEstimate(
            flops=2 * 1024 * 128 * 128, bytes_accessed=1 << 20, transcendentals=1 << 18
        ),
    )(
        normed,
        *in_hbm(w_gate, w_out, ln_out_gain.reshape(1, 128), ln_out_bias.reshape(1, 128)),
    )
    gate, keep = lax.optimization_barrier((gate, keep))
    triangle = call(add_halves, shape(4, 2, 4, 4, 8, 128), [VMEM] * 2)(keep, got)
    triangle = lax.all_to_all(triangle.reshape(128, 8, 128), PEERS, 0, 0, tiled=True)
    return call(
        finish,
        shape(16, 64, 128),
        [VMEM] * 4,
        [
            pltpu.VMEM((1024, 128), F32),
            pltpu.VMEM((16, 64, 128), BF16),
            pltpu.SemaphoreType.DMA((4,)),
        ],
        out_spec=HBM,
    )(triangle, gate, w_out, affine)


def solution(mesh):
    fine = Mesh(mesh.devices.reshape(4, 2, 4, 4, 2), ("y", "zh", "x", "zl", "core"))
    tile = P(("y", "zh", "x"), ("zl", "core"), None)
    return jax.shard_map(
        shards, mesh=fine, in_specs=(tile,) + (P(),) * 11, out_specs=tile, check_vma=False
    )
```

```python
import jax
import jax.numpy as jnp
from jax import lax
from jax.experimental import pallas as pl
from jax.experimental.pallas import tpu as pltpu
from jax.sharding import Mesh, PartitionSpec as P

F32 = jnp.float32
BF16 = jnp.bfloat16
NT = (((1,), (1,)), ((), ()))
TN = (((0,), (0,)), ((), ()))
MIB = 1024 * 1024
VMEM = pl.BlockSpec(memory_space=pltpu.VMEM)
HBM = pl.BlockSpec(memory_space=pltpu.HBM)
PEERS = ("zl", "zh", "y", "x")


def low_lanes(shape):
    return lax.broadcasted_iota(jnp.int32, shape, len(shape) - 1) < 64


def fetch(sources, targets, sems):
    copies = [
        pltpu.make_async_copy(source, target, sems.at[n])
        for n, (source, target) in enumerate(zip(sources, targets))
    ]
    for copy in copies:
        copy.start()
    return copies


def project(
    x_hbm, mask_flat, mask_rows, gain_hbm, bias_hbm, w_l, w_lg, w_r, w_rg,
    out_ref, normed_ref,
    x_ref, mask_scalars, mask_ref, gain, bias, w_ref, rows, sems,
):
    copies = fetch(
        (x_hbm, gain_hbm, bias_hbm, mask_flat, mask_rows, w_l, w_lg, w_r, w_rg),
        (x_ref, gain, bias, mask_scalars, mask_ref) + tuple(w_ref.at[n] for n in range(4)),
        sems,
    )
    row = lax.axis_index("y") * 8 + lax.axis_index("zh") * 4 + lax.axis_index("x")
    core = lax.axis_index("core")
    for copy in copies:
        copy.wait()
    weights = jnp.concatenate([w_ref[n].T for n in range(4)], axis=0)
    mask_all = mask_ref[...].astype(F32)
    mask_k = mask_all[:1]
    for z in range(1, 4):
        mask_k = jnp.where(lax.axis_index("zl") == z, mask_all[z : z + 1], mask_k)
    swapped = pltpu.roll(mask_k, 64, 1)
    low = low_lanes((1, 128))
    mask_k = jnp.where(low == (core == 0), mask_k, swapped)
    for first in range(0, 8, 2):
        parts = []
        for start in (first, first + 8):
            x = x_ref[start : start + 2].astype(F32)
            centred = x - jnp.mean(x, axis=-1, keepdims=True)
            variance = jnp.mean(centred * centred, axis=-1, keepdims=True)
            part = centred * lax.rsqrt(variance + 1e-05) * gain[...] + bias[...]
            parts.append(part.astype(BF16))
            normed_ref[start : start + 2] = parts[-1]
        tokens = jnp.stack(parts, axis=1).reshape(128 * 2, 128)
        projected = lax.dot_general(weights, tokens, NT, preferred_element_type=F32)
        for n in range(2):
            s = first + n
            p = projected[:, 128 * n : 128 * n + 128]
            mask_a = mask_scalars[row * 16 + s].astype(F32)
            mask_b = mask_scalars[row * 16 + s + 8].astype(F32)
            mask = mask_k * jnp.where(low, mask_a, mask_b)
            left = mask * jax.nn.sigmoid(p[128:256]) * p[:128]
            right = mask * jax.nn.sigmoid(p[384:]) * p[256:384]
            rows[pl.ds(s, 128, stride=8), :] = left
            rows[pl.ds(1024 + s, 128, stride=8), :] = right
    left = rows[:1024].reshape(128, 8, 128)
    right = rows[1024:2048].reshape(128, 8, 128)
    out_ref[...] = jnp.concatenate([left, right], axis=1).astype(BF16)


def contract(s_ref, keep_ref, send_ref):
    core = lax.axis_index("core")
    edges = s_ref[...].astype(F32).reshape(4, 2, 4, 4, 16, 128)
    edges = jnp.stack([edges[:, 0], edges[:, 1]], axis=2).reshape(4, 32, 16, 128)
    low = low_lanes((256, 128))

    def halves(part):
        first, second = [], []
        for z in (0, 2):
            a, b = part(z), part(z + 1)
            first.append(jnp.where(low, a, pltpu.roll(b, 64, 1)).astype(BF16))
            second.append(jnp.where(low, pltpu.roll(a, 64, 1), b).astype(BF16))
        return jnp.concatenate(first, axis=1), jnp.concatenate(second, axis=1)

    left = jnp.concatenate(halves(lambda z: edges[z, :, :8].reshape(256, 128)), axis=0)
    right = halves(lambda z: edges[z, :, 8:].reshape(256, 128))
    both = jnp.concatenate([r.reshape(4, 2, 32, 256) for r in right], axis=2)
    first, second = both[:, 0].reshape(256, 256), both[:, 1].reshape(256, 256)
    mine = jnp.where(core == 0, first, second)
    other = jnp.where(core == 0, second, first)
    send_ref[...] = lax.dot_general(left, other, NT, preferred_element_type=F32).astype(BF16)
    keep_ref[...] = lax.dot_general(left, mine, NT, preferred_element_type=F32)


def prepare(
    normed_ref, w_gate, w_out_hbm, gain_hbm, bias_hbm,
    gate_ref, w_out_ref, affine_ref,
    w_ref, gain, bias, sems,
):
    copies = fetch(
        (w_gate, w_out_hbm, gain_hbm, bias_hbm), (w_ref, w_out_ref, gain, bias), sems
    )
    for copy in copies:
        copy.wait()
    flat = normed_ref[...].reshape(1024, 128)
    gate = jax.nn.sigmoid(jnp.dot(flat, w_ref[...], preferred_element_type=F32))
    gate_ref[...] = gate.reshape(16, 64, 128)
    affine_ref[0] = jnp.broadcast_to(gain[...], (128, 128)).T
    affine_ref[1] = jnp.broadcast_to(bias[...], (128, 128)).T


def add_halves(keep_ref, got_ref, out_ref):
    low = low_lanes((256, 128))
    for v in range(2):
        cols = slice(128 * v, 128 * v + 128)
        a = keep_ref[:256, cols] + got_ref[:256, cols].astype(F32)
        b = keep_ref[256:, cols] + got_ref[256:, cols].astype(F32)
        even = jnp.where(low, a, pltpu.roll(b, 64, 1))
        odd = jnp.where(low, pltpu.roll(a, 64, 1), b)
        even = even.reshape(4, 2, 4, 8, 128).astype(BF16)
        odd = odd.reshape(4, 2, 4, 8, 128).astype(BF16)
        for zh in range(2):
            out_ref[2 * v, zh] = even[:, zh]
            out_ref[2 * v + 1, zh] = odd[:, zh]


def finish(t_ref, gate_ref, w_out, affine, out_hbm, rows, out_ref, sems):
    t = t_ref[...].astype(F32)
    rows[:1024] = t.reshape(1024, 128)
    gain_col, bias_col = affine[0], affine[1]
    w = w_out[...]
    copies = []
    for s in range(8):
        n = rows[pl.ds(s, 128, stride=8), :]
        n = n - jnp.mean(n, axis=0, keepdims=True)
        variance = jnp.mean(n * n, axis=0, keepdims=True)
        n = (n * lax.rsqrt(variance + 1e-05) * gain_col + bias_col).astype(BF16)
        y = lax.dot_general(n, w, TN, preferred_element_type=F32).reshape(2, 2, 4, 8, 128)
        for b in range(2):
            i = s + 8 * b
            token = jnp.stack([y[b, 0], y[b, 1]], axis=1).reshape(64, 128)
            out_ref[i] = (gate_ref[i] * token).astype(BF16)
        if s % 4 == 3:
            for b in range(2):
                part = pl.ds(s - 3 + 8 * b, 4)
                copies.append(
                    pltpu.make_async_copy(
                        out_ref.at[part], out_hbm.at[part], sems.at[len(copies)]
                    )
                )
                copies[-1].start()
    for copy in copies:
        copy.wait()


def call(kernel, outs, specs, scratch=(), out_spec=VMEM, cost=None, limit=24):
    return pl.pallas_call(
        kernel,
        out_shape=outs,
        in_specs=specs,
        out_specs=jax.tree.map(lambda _: out_spec, outs),
        scratch_shapes=scratch,
        compiler_params=pltpu.CompilerParams(vmem_limit_bytes=limit * MIB),
        cost_estimate=cost,
    )


def in_hbm(*arrays):
    return [pltpu.with_memory_space_constraint(a, pltpu.HBM) for a in arrays]


def shape(*dims, dtype=BF16):
    return jax.ShapeDtypeStruct(dims, dtype)


def shards(
    pair,
    token_mask,
    ln_in_gain,
    ln_in_bias,
    w_left,
    w_left_gate,
    w_right,
    w_right_gate,
    w_gate,
    ln_out_gain,
    ln_out_bias,
    w_out,
):
    edges, normed = call(
        project,
        (shape(128, 16, 128), shape(16, 64, 128)),
        [HBM] * 9,
        [
            pltpu.VMEM((16, 64, 128), BF16),
            pltpu.SMEM((512,), jnp.int32),
            pltpu.VMEM((4, 128), jnp.int32),
            pltpu.VMEM((1, 128), F32),
            pltpu.VMEM((1, 128), F32),
            pltpu.VMEM((4, 128, 128), BF16),
            pltpu.VMEM((2056, 128), F32),
            pltpu.SemaphoreType.DMA((9,)),
        ],
    )(
        *in_hbm(
            pair,
            token_mask,
            token_mask.reshape(4, 128),
            ln_in_gain.reshape(1, 128),
            ln_in_bias.reshape(1, 128),
            w_left,
            w_left_gate,
            w_right,
            w_right_gate,
        )
    )
    edges = lax.all_to_all(edges, PEERS, 0, 0, tiled=True)
    keep, send = call(contract, (shape(512, 256, dtype=F32), shape(512, 256)), [VMEM])(edges)
    got = lax.ppermute(send, "core", [(0, 1), (1, 0)])
    normed, keep = lax.optimization_barrier((normed, keep))
    gate, w_out, affine = call(
        prepare,
        (shape(16, 64, 128, dtype=F32), shape(128, 128), shape(2, 128, 128, dtype=F32)),
        [VMEM] + [HBM] * 4,
        [
            pltpu.VMEM((128, 128), BF16),
            pltpu.VMEM((1, 128), F32),
            pltpu.VMEM((1, 128), F32),
            pltpu.SemaphoreType.DMA((4,)),
        ],
        cost=pl.CostEstimate(
            flops=2 * 1024 * 128 * 128, bytes_accessed=1 << 20, transcendentals=1 << 18
        ),
    )(
        normed,
        *in_hbm(w_gate, w_out, ln_out_gain.reshape(1, 128), ln_out_bias.reshape(1, 128)),
    )
    gate, keep = lax.optimization_barrier((gate, keep))
    triangle = call(add_halves, shape(4, 2, 4, 4, 8, 128), [VMEM] * 2)(keep, got)
    triangle = lax.all_to_all(triangle.reshape(128, 8, 128), PEERS, 0, 0, tiled=True)
    return call(
        finish,
        shape(16, 64, 128),
        [VMEM] * 4,
        [
            pltpu.VMEM((1032, 128), F32),
            pltpu.VMEM((16, 64, 128), BF16),
            pltpu.SemaphoreType.DMA((4,)),
        ],
        out_spec=HBM,
    )(triangle, gate, w_out, affine)


def solution(mesh):
    fine = Mesh(mesh.devices.reshape(4, 2, 4, 4, 2), ("y", "zh", "x", "zl", "core"))
    tile = P(("y", "zh", "x"), ("zl", "core"), None)
    return jax.shard_map(
        shards, mesh=fine, in_specs=(tile,) + (P(),) * 11, out_specs=tile, check_vma=False
    )
```

```python
import jax
import jax.numpy as jnp
from jax import lax
from jax.experimental import pallas as pl
from jax.experimental.pallas import tpu as pltpu
from jax.sharding import Mesh, PartitionSpec as P

F32 = jnp.float32
BF16 = jnp.bfloat16
NT = (((1,), (1,)), ((), ()))
TN = (((0,), (0,)), ((), ()))
MIB = 1024 * 1024
VMEM = pl.BlockSpec(memory_space=pltpu.VMEM)
HBM = pl.BlockSpec(memory_space=pltpu.HBM)
PEERS = ("zl", "zh", "y", "x")


def low_lanes(shape):
    return lax.broadcasted_iota(jnp.int32, shape, len(shape) - 1) < 64


def fetch(sources, targets, sems):
    copies = [
        pltpu.make_async_copy(source, target, sems.at[n])
        for n, (source, target) in enumerate(zip(sources, targets))
    ]
    for copy in copies:
        copy.start()
    return copies


def project(
    x_hbm, mask_flat, mask_rows, gain_hbm, bias_hbm, w_l, w_lg, w_r, w_rg,
    out_ref, normed_ref,
    x_ref, mask_scalars, mask_ref, gain, bias, w_ref, rows, sems,
):
    copies = fetch(
        (x_hbm, gain_hbm, bias_hbm, mask_flat, mask_rows, w_l, w_lg, w_r, w_rg),
        (x_ref, gain, bias, mask_scalars, mask_ref) + tuple(w_ref.at[n] for n in range(4)),
        sems,
    )
    row = lax.axis_index("y") * 8 + lax.axis_index("zh") * 4 + lax.axis_index("x")
    core = lax.axis_index("core")
    for copy in copies:
        copy.wait()
    weights = jnp.concatenate([w_ref[n].T for n in range(4)], axis=0)
    mask_all = mask_ref[...].astype(F32)
    mask_k = mask_all[:1]
    for z in range(1, 4):
        mask_k = jnp.where(lax.axis_index("zl") == z, mask_all[z : z + 1], mask_k)
    swapped = pltpu.roll(mask_k, 64, 1)
    low = low_lanes((1, 128))
    mask_k = jnp.where(low == (core == 0), mask_k, swapped)
    for first in range(0, 8, 2):
        parts = []
        for start in (first, first + 8):
            x = x_ref[start : start + 2].astype(F32)
            centred = x - jnp.mean(x, axis=-1, keepdims=True)
            variance = jnp.mean(centred * centred, axis=-1, keepdims=True)
            part = centred * lax.rsqrt(variance + 1e-05) * gain[...] + bias[...]
            parts.append(part.astype(BF16))
            normed_ref[start : start + 2] = parts[-1]
        tokens = jnp.stack(parts, axis=1).reshape(128 * 2, 128)
        projected = lax.dot_general(weights, tokens, NT, preferred_element_type=F32)
        for n in range(2):
            s = first + n
            p = projected[:, 128 * n : 128 * n + 128]
            mask_a = mask_scalars[row * 16 + s].astype(F32)
            mask_b = mask_scalars[row * 16 + s + 8].astype(F32)
            mask = mask_k * jnp.where(low, mask_a, mask_b)
            left = mask * jax.nn.sigmoid(p[128:256]) * p[:128]
            right = mask * jax.nn.sigmoid(p[384:]) * p[256:384]
            rows[pl.ds(s, 128, stride=8), :] = left
            rows[pl.ds(1024 + s, 128, stride=8), :] = right
    left = rows[:1024].reshape(128, 8, 128)
    right = rows[1024:2048].reshape(128, 8, 128)
    out_ref[...] = jnp.concatenate([left, right], axis=1).astype(BF16)


def contract(s_ref, send_ref, left_ref, mine_ref):
    core = lax.axis_index("core")
    edges = s_ref[...].astype(F32).reshape(4, 2, 4, 4, 16, 128)
    edges = jnp.stack([edges[:, 0], edges[:, 1]], axis=2).reshape(4, 32, 16, 128)
    low = low_lanes((256, 128))

    def halves(part):
        first, second = [], []
        for z in (0, 2):
            a, b = part(z), part(z + 1)
            first.append(jnp.where(low, a, pltpu.roll(b, 64, 1)).astype(BF16))
            second.append(jnp.where(low, pltpu.roll(a, 64, 1), b).astype(BF16))
        return jnp.concatenate(first, axis=1), jnp.concatenate(second, axis=1)

    left = jnp.concatenate(halves(lambda z: edges[z, :, :8].reshape(256, 128)), axis=0)
    right = halves(lambda z: edges[z, :, 8:].reshape(256, 128))
    both = jnp.concatenate([r.reshape(4, 2, 32, 256) for r in right], axis=2)
    first, second = both[:, 0].reshape(256, 256), both[:, 1].reshape(256, 256)
    left_ref[...] = left
    mine_ref[...] = jnp.where(core == 0, first, second)
    other = jnp.where(core == 0, second, first)
    send_ref[...] = lax.dot_general(left, other, NT, preferred_element_type=F32).astype(BF16)


def prepare(
    left_ref, mine_ref, normed_ref, w_gate, w_out_hbm, gain_hbm, bias_hbm,
    keep_ref, gate_ref, w_out_ref, affine_ref,
    w_ref, gain, bias, sems,
):
    copies = fetch(
        (w_gate, w_out_hbm, gain_hbm, bias_hbm), (w_ref, w_out_ref, gain, bias), sems
    )
    keep_ref[...] = lax.dot_general(
        left_ref[...], mine_ref[...], NT, preferred_element_type=F32
    )
    for copy in copies:
        copy.wait()
    flat = normed_ref[...].reshape(1024, 128)
    gate = jax.nn.sigmoid(jnp.dot(flat, w_ref[...], preferred_element_type=F32))
    gate_ref[...] = gate.reshape(16, 64, 128)
    affine_ref[0] = jnp.broadcast_to(gain[...], (128, 128)).T
    affine_ref[1] = jnp.broadcast_to(bias[...], (128, 128)).T


def add_halves(keep_ref, got_ref, out_ref):
    low = low_lanes((256, 128))
    for v in range(2):
        cols = slice(128 * v, 128 * v + 128)
        a = keep_ref[:256, cols] + got_ref[:256, cols].astype(F32)
        b = keep_ref[256:, cols] + got_ref[256:, cols].astype(F32)
        even = jnp.where(low, a, pltpu.roll(b, 64, 1))
        odd = jnp.where(low, pltpu.roll(a, 64, 1), b)
        even = even.reshape(4, 2, 4, 8, 128).astype(BF16)
        odd = odd.reshape(4, 2, 4, 8, 128).astype(BF16)
        for zh in range(2):
            out_ref[2 * v, zh] = even[:, zh]
            out_ref[2 * v + 1, zh] = odd[:, zh]


def finish(t_ref, gate_ref, w_out, affine, out_hbm, rows, out_ref, sems):
    t = t_ref[...].astype(F32)
    rows[:1024] = t.reshape(1024, 128)
    gain_col, bias_col = affine[0], affine[1]
    w = w_out[...]
    copies = []
    for s in range(8):
        n = rows[pl.ds(s, 128, stride=8), :]
        n = n - jnp.mean(n, axis=0, keepdims=True)
        variance = jnp.mean(n * n, axis=0, keepdims=True)
        n = (n * lax.rsqrt(variance + 1e-05) * gain_col + bias_col).astype(BF16)
        y = lax.dot_general(n, w, TN, preferred_element_type=F32).reshape(2, 2, 4, 8, 128)
        for b in range(2):
            i = s + 8 * b
            token = jnp.stack([y[b, 0], y[b, 1]], axis=1).reshape(64, 128)
            out_ref[i] = (gate_ref[i] * token).astype(BF16)
        if s % 4 == 3:
            for b in range(2):
                part = pl.ds(s - 3 + 8 * b, 4)
                copies.append(
                    pltpu.make_async_copy(
                        out_ref.at[part], out_hbm.at[part], sems.at[len(copies)]
                    )
                )
                copies[-1].start()
    for copy in copies:
        copy.wait()


def call(kernel, outs, specs, scratch=(), out_spec=VMEM, cost=None, limit=24):
    return pl.pallas_call(
        kernel,
        out_shape=outs,
        in_specs=specs,
        out_specs=jax.tree.map(lambda _: out_spec, outs),
        scratch_shapes=scratch,
        compiler_params=pltpu.CompilerParams(vmem_limit_bytes=limit * MIB),
        cost_estimate=cost,
    )


def in_hbm(*arrays):
    return [pltpu.with_memory_space_constraint(a, pltpu.HBM) for a in arrays]


def shape(*dims, dtype=BF16):
    return jax.ShapeDtypeStruct(dims, dtype)


def shards(
    pair,
    token_mask,
    ln_in_gain,
    ln_in_bias,
    w_left,
    w_left_gate,
    w_right,
    w_right_gate,
    w_gate,
    ln_out_gain,
    ln_out_bias,
    w_out,
):
    edges, normed = call(
        project,
        (shape(128, 16, 128), shape(16, 64, 128)),
        [HBM] * 9,
        [
            pltpu.VMEM((16, 64, 128), BF16),
            pltpu.SMEM((512,), jnp.int32),
            pltpu.VMEM((4, 128), jnp.int32),
            pltpu.VMEM((1, 128), F32),
            pltpu.VMEM((1, 128), F32),
            pltpu.VMEM((4, 128, 128), BF16),
            pltpu.VMEM((2056, 128), F32),
            pltpu.SemaphoreType.DMA((9,)),
        ],
    )(
        *in_hbm(
            pair,
            token_mask,
            token_mask.reshape(4, 128),
            ln_in_gain.reshape(1, 128),
            ln_in_bias.reshape(1, 128),
            w_left,
            w_left_gate,
            w_right,
            w_right_gate,
        )
    )
    edges = lax.all_to_all(edges, PEERS, 0, 0, tiled=True)
    send, left, mine = call(
        contract, (shape(512, 256), shape(512, 256), shape(256, 256)), [VMEM]
    )(edges)
    got = lax.ppermute(send, "core", [(0, 1), (1, 0)])
    keep, gate, w_out, affine = call(
        prepare,
        (
            shape(512, 256, dtype=F32),
            shape(16, 64, 128, dtype=F32),
            shape(128, 128),
            shape(2, 128, 128, dtype=F32),
        ),
        [VMEM] * 3 + [HBM] * 4,
        [
            pltpu.VMEM((128, 128), BF16),
            pltpu.VMEM((1, 128), F32),
            pltpu.VMEM((1, 128), F32),
            pltpu.SemaphoreType.DMA((4,)),
        ],
        cost=pl.CostEstimate(
            flops=2 * 1024 * 128 * 128 + 2 * 512 * 256 * 256, bytes_accessed=1 << 20, transcendentals=1 << 18
        ),
    )(
        left,
        mine,
        normed,
        *in_hbm(w_gate, w_out, ln_out_gain.reshape(1, 128), ln_out_bias.reshape(1, 128)),
    )
    triangle = call(add_halves, shape(4, 2, 4, 4, 8, 128), [VMEM] * 2)(keep, got)
    triangle = lax.all_to_all(triangle.reshape(128, 8, 128), PEERS, 0, 0, tiled=True)
    return call(
        finish,
        shape(16, 64, 128),
        [VMEM] * 4,
        [
            pltpu.VMEM((1032, 128), F32),
            pltpu.VMEM((16, 64, 128), BF16),
            pltpu.SemaphoreType.DMA((4,)),
        ],
        out_spec=HBM,
    )(triangle, gate, w_out, affine)


def solution(mesh):
    fine = Mesh(mesh.devices.reshape(4, 2, 4, 4, 2), ("y", "zh", "x", "zl", "core"))
    tile = P(("y", "zh", "x"), ("zl", "core"), None)
    return jax.shard_map(
        shards, mesh=fine, in_specs=(tile,) + (P(),) * 11, out_specs=tile, check_vma=False
    )
```

```python
import jax
import jax.numpy as jnp
from jax import lax
from jax.experimental import pallas as pl
from jax.experimental.pallas import tpu as pltpu
from jax.sharding import Mesh, PartitionSpec as P

F32 = jnp.float32
BF16 = jnp.bfloat16
NT = (((1,), (1,)), ((), ()))
TN = (((0,), (0,)), ((), ()))
MIB = 1024 * 1024
VMEM = pl.BlockSpec(memory_space=pltpu.VMEM)
HBM = pl.BlockSpec(memory_space=pltpu.HBM)
PEERS = ("zl", "zh", "y", "x")


def low_lanes(shape):
    return lax.broadcasted_iota(jnp.int32, shape, len(shape) - 1) < 64


def fetch(sources, targets, sems):
    copies = [
        pltpu.make_async_copy(source, target, sems.at[n])
        for n, (source, target) in enumerate(zip(sources, targets))
    ]
    for copy in copies:
        copy.start()
    return copies


def project(
    x_hbm, mask_flat, mask_rows, gain_hbm, bias_hbm, w_l, w_lg, w_r, w_rg,
    out_ref, normed_ref,
    x_ref, mask_scalars, mask_ref, gain, bias, w_ref, rows, sems,
):
    copies = fetch(
        (x_hbm, gain_hbm, bias_hbm, mask_flat, mask_rows, w_l, w_lg, w_r, w_rg),
        (x_ref, gain, bias, mask_scalars, mask_ref) + tuple(w_ref.at[n] for n in range(4)),
        sems,
    )
    row = lax.axis_index("y") * 8 + lax.axis_index("zh") * 4 + lax.axis_index("x")
    core = lax.axis_index("core")
    for copy in copies:
        copy.wait()
    weights = jnp.concatenate([w_ref[n].T for n in range(4)], axis=0)
    mask_all = mask_ref[...].astype(F32)
    mask_k = mask_all[:1]
    for z in range(1, 4):
        mask_k = jnp.where(lax.axis_index("zl") == z, mask_all[z : z + 1], mask_k)
    swapped = pltpu.roll(mask_k, 64, 1)
    low = low_lanes((1, 128))
    mask_k = jnp.where(low == (core == 0), mask_k, swapped)
    for first in range(0, 8, 2):
        parts = []
        for start in (first, first + 8):
            x = x_ref[start : start + 2].astype(F32)
            centred = x - jnp.mean(x, axis=-1, keepdims=True)
            variance = jnp.mean(centred * centred, axis=-1, keepdims=True)
            part = centred * lax.rsqrt(variance + 1e-05) * gain[...] + bias[...]
            parts.append(part.astype(BF16))
            normed_ref[start : start + 2] = parts[-1]
        tokens = jnp.stack(parts, axis=1).reshape(128 * 2, 128)
        projected = lax.dot_general(weights, tokens, NT, preferred_element_type=F32)
        for n in range(2):
            s = first + n
            p = projected[:, 128 * n : 128 * n + 128]
            mask_a = mask_scalars[row * 16 + s].astype(F32)
            mask_b = mask_scalars[row * 16 + s + 8].astype(F32)
            mask = mask_k * jnp.where(low, mask_a, mask_b)
            left = mask * jax.nn.sigmoid(p[128:256]) * p[:128]
            right = mask * jax.nn.sigmoid(p[384:]) * p[256:384]
            rows[pl.ds(s, 128, stride=8), :] = left
            rows[pl.ds(1024 + s, 128, stride=8), :] = right
    left = rows[:1024].reshape(128, 8, 128)
    right = rows[1024:2048].reshape(128, 8, 128)
    out_ref[...] = jnp.concatenate([left, right], axis=1).astype(BF16)


def arrived(s_ref):
    edges = s_ref[...].astype(F32).reshape(4, 2, 4, 4, 16, 128)
    return jnp.stack([edges[:, 0], edges[:, 1]], axis=2)


def halves(part):
    first, second = [], []
    for z in (0, 2):
        a, b = part(z), part(z + 1)
        low = low_lanes(a.shape)
        first.append(jnp.where(low, a, pltpu.roll(b, 64, 1)).astype(BF16))
        second.append(jnp.where(low, pltpu.roll(a, 64, 1), b).astype(BF16))
    return jnp.concatenate(first, axis=1), jnp.concatenate(second, axis=1)


def right_rows(edges, first_half):
    def part(z):
        rows = jnp.where(first_half, edges[z, :, 0, :, 8:], edges[z, :, 1, :, 8:])
        return rows.reshape(128, 128)

    pair = [half.reshape(4, 32, 256) for half in halves(part)]
    return jnp.concatenate(pair, axis=1).reshape(256, 256)


def contract(s_ref, send_ref, left_ref):
    edges = arrived(s_ref)
    left = jnp.concatenate(halves(lambda z: edges[z, :, :, :, :8].reshape(256, 128)), axis=0)
    left_ref[...] = left
    other = right_rows(edges, lax.axis_index("core") == 1)
    send_ref[...] = lax.dot_general(left, other, NT, preferred_element_type=F32).astype(BF16)


def prepare(
    left_ref, s_ref, normed_ref, w_gate, w_out_hbm, gain_hbm, bias_hbm,
    keep_ref, gate_ref, w_out_ref, affine_ref,
    w_ref, gain, bias, sems,
):
    copies = fetch(
        (w_gate, w_out_hbm, gain_hbm, bias_hbm), (w_ref, w_out_ref, gain, bias), sems
    )
    mine = right_rows(arrived(s_ref), lax.axis_index("core") == 0)
    keep_ref[...] = lax.dot_general(left_ref[...], mine, NT, preferred_element_type=F32)
    for copy in copies:
        copy.wait()
    flat = normed_ref[...].reshape(1024, 128)
    gate = jax.nn.sigmoid(jnp.dot(flat, w_ref[...], preferred_element_type=F32))
    gate_ref[...] = gate.reshape(16, 64, 128)
    affine_ref[0] = jnp.broadcast_to(gain[...], (128, 128)).T
    affine_ref[1] = jnp.broadcast_to(bias[...], (128, 128)).T


def add_halves(keep_ref, got_ref, out_ref):
    low = low_lanes((256, 128))
    for v in range(2):
        cols = slice(128 * v, 128 * v + 128)
        a = keep_ref[:256, cols] + got_ref[:256, cols].astype(F32)
        b = keep_ref[256:, cols] + got_ref[256:, cols].astype(F32)
        even = jnp.where(low, a, pltpu.roll(b, 64, 1))
        odd = jnp.where(low, pltpu.roll(a, 64, 1), b)
        even = even.reshape(4, 2, 4, 8, 128).astype(BF16)
        odd = odd.reshape(4, 2, 4, 8, 128).astype(BF16)
        for zh in range(2):
            out_ref[2 * v, zh] = even[:, zh]
            out_ref[2 * v + 1, zh] = odd[:, zh]


def finish(t_ref, gate_ref, w_out, affine, out_hbm, rows, out_ref, sems):
    t = t_ref[...].astype(F32)
    rows[:1024] = t.reshape(1024, 128)
    gain_col, bias_col = affine[0], affine[1]
    w = w_out[...]
    copies = []
    for s in range(8):
        n = rows[pl.ds(s, 128, stride=8), :]
        n = n - jnp.mean(n, axis=0, keepdims=True)
        variance = jnp.mean(n * n, axis=0, keepdims=True)
        n = (n * lax.rsqrt(variance + 1e-05) * gain_col + bias_col).astype(BF16)
        y = lax.dot_general(n, w, TN, preferred_element_type=F32).reshape(2, 2, 4, 8, 128)
        for b in range(2):
            i = s + 8 * b
            token = jnp.stack([y[b, 0], y[b, 1]], axis=1).reshape(64, 128)
            out_ref[i] = (gate_ref[i] * token).astype(BF16)
        if s % 4 == 3:
            for b in range(2):
                part = pl.ds(s - 3 + 8 * b, 4)
                copies.append(
                    pltpu.make_async_copy(
                        out_ref.at[part], out_hbm.at[part], sems.at[len(copies)]
                    )
                )
                copies[-1].start()
    for copy in copies:
        copy.wait()


def call(kernel, outs, specs, scratch=(), out_spec=VMEM, cost=None, limit=24):
    return pl.pallas_call(
        kernel,
        out_shape=outs,
        in_specs=specs,
        out_specs=jax.tree.map(lambda _: out_spec, outs),
        scratch_shapes=scratch,
        compiler_params=pltpu.CompilerParams(vmem_limit_bytes=limit * MIB),
        cost_estimate=cost,
    )


def in_hbm(*arrays):
    return [pltpu.with_memory_space_constraint(a, pltpu.HBM) for a in arrays]


def shape(*dims, dtype=BF16):
    return jax.ShapeDtypeStruct(dims, dtype)


def shards(
    pair,
    token_mask,
    ln_in_gain,
    ln_in_bias,
    w_left,
    w_left_gate,
    w_right,
    w_right_gate,
    w_gate,
    ln_out_gain,
    ln_out_bias,
    w_out,
):
    edges, normed = call(
        project,
        (shape(128, 16, 128), shape(16, 64, 128)),
        [HBM] * 9,
        [
            pltpu.VMEM((16, 64, 128), BF16),
            pltpu.SMEM((512,), jnp.int32),
            pltpu.VMEM((4, 128), jnp.int32),
            pltpu.VMEM((1, 128), F32),
            pltpu.VMEM((1, 128), F32),
            pltpu.VMEM((4, 128, 128), BF16),
            pltpu.VMEM((2056, 128), F32),
            pltpu.SemaphoreType.DMA((9,)),
        ],
    )(
        *in_hbm(
            pair,
            token_mask,
            token_mask.reshape(4, 128),
            ln_in_gain.reshape(1, 128),
            ln_in_bias.reshape(1, 128),
            w_left,
            w_left_gate,
            w_right,
            w_right_gate,
        )
    )
    edges = lax.all_to_all(edges, PEERS, 0, 0, tiled=True)
    send, left = call(contract, (shape(512, 256), shape(512, 256)), [VMEM])(edges)
    got = lax.ppermute(send, "core", [(0, 1), (1, 0)])
    keep, gate, w_out, affine = call(
        prepare,
        (
            shape(512, 256, dtype=F32),
            shape(16, 64, 128, dtype=F32),
            shape(128, 128),
            shape(2, 128, 128, dtype=F32),
        ),
        [VMEM] * 3 + [HBM] * 4,
        [
            pltpu.VMEM((128, 128), BF16),
            pltpu.VMEM((1, 128), F32),
            pltpu.VMEM((1, 128), F32),
            pltpu.SemaphoreType.DMA((4,)),
        ],
        cost=pl.CostEstimate(
            flops=2 * 1024 * 128 * 128 + 2 * 512 * 256 * 256, bytes_accessed=1 << 20, transcendentals=1 << 18
        ),
    )(
        left,
        edges,
        normed,
        *in_hbm(w_gate, w_out, ln_out_gain.reshape(1, 128), ln_out_bias.reshape(1, 128)),
    )
    triangle = call(add_halves, shape(4, 2, 4, 4, 8, 128), [VMEM] * 2)(keep, got)
    triangle = lax.all_to_all(triangle.reshape(128, 8, 128), PEERS, 0, 0, tiled=True)
    return call(
        finish,
        shape(16, 64, 128),
        [VMEM] * 4,
        [
            pltpu.VMEM((1032, 128), F32),
            pltpu.VMEM((16, 64, 128), BF16),
            pltpu.SemaphoreType.DMA((4,)),
        ],
        out_spec=HBM,
    )(triangle, gate, w_out, affine)


def solution(mesh):
    fine = Mesh(mesh.devices.reshape(4, 2, 4, 4, 2), ("y", "zh", "x", "zl", "core"))
    tile = P(("y", "zh", "x"), ("zl", "core"), None)
    return jax.shard_map(
        shards, mesh=fine, in_specs=(tile,) + (P(),) * 11, out_specs=tile, check_vma=False
    )
```
